256 devices in a mesh: frame: 64 (over x, z, core), space: 4 (over y).
Axes of the slice: x: 4, y: 4, z: 8, core: 2. Of those that a mesh axis runs over, the one named last changes fastest.
Arguments:
- queries: bfloat16 [64, 2048, 1152], P('frame', 'space'), may hold values from -2 to 2
- keys: bfloat16 [64, 2048, 1152], P('frame', 'space'), may hold values from -6 to 6
- values: bfloat16 [64, 2048, 1152], P('frame', 'space'), may hold values from -6 to 6
- cotangent: bfloat16 [64, 2048, 1152], P('frame', 'space'), may hold values from -6 to 6
Outputs:
- grad_queries: bfloat16 [64, 2048, 1152], P('frame', 'space')
- grad_keys: bfloat16 [64, 2048, 1152], P('frame', 'space')
- grad_values: bfloat16 [64, 2048, 1152], P('frame', 'space')
The draws below stay inside these ranges and needn't reach their ends.
All inputs are finite; a program needn't handle non-finite values.
Results may differ from the reference program's by a relative error of at most 0.003.
Values sent between devices are 32-bit elements; how exact they have to be, the bound alone decides.
No kernel may reach another device: no remote copies, remote signals or barrier semaphores. Data moves between devices by JAX's collectives and lax.ppermute only.
A program may use at most 192 MiB of HBM per device.

```python
import jax
import jax.numpy as jnp
from jax import lax

HEADS = 36
HEAD_DIM = 32
CH = 1152
FRAMES = 64
FRAME_TOK = 2048


def frame_level(key, reach):
    sign_key, jitter_key = jax.random.split(key)
    direction = (jax.random.randint(sign_key, (1,), 0, 2) * 2 - 1).astype(jnp.float32)
    position = 2.0 * jnp.arange(FRAMES, dtype=jnp.float32) / max(FRAMES - 1, 1) - 1.0
    jitter = jax.random.uniform(jitter_key, (FRAMES,), jnp.float32, -0.5, 0.5)
    return jnp.exp(reach * (0.8 * direction * position + jitter)).reshape(FRAMES, 1, 1)


def token_noise(key):
    noise_key = jax.random.fold_in(key, 0)
    return jax.random.normal(noise_key, (FRAMES, FRAME_TOK, CH), jnp.float32)


def offset_rows(key, spread, reach):
    mean_key, shift_key, level_key, noise_key = jax.random.split(key, 4)
    channel_mean = jax.random.normal(mean_key, (CH,), jnp.float32)
    frame_shift = 0.8 * jax.random.normal(shift_key, (FRAMES, 1, CH), jnp.float32)
    level = frame_level(level_key, reach)
    whole = (channel_mean[None, None, :] * spread + frame_shift + token_noise(noise_key)) * level
    return jnp.clip(whole, -6.0, 6.0).astype(jnp.bfloat16)


def draw_queries(key, part):
    key = jax.random.fold_in(key, 7)
    level_key, noise_key = jax.random.split(key)
    whole = 0.3 * frame_level(level_key, 1.0) * token_noise(noise_key)
    return jnp.clip(whole, -2.0, 2.0).astype(jnp.bfloat16)


def draw_keys(key, part):
    key = jax.random.fold_in(key, 5)
    level_key, noise_key = jax.random.split(key)
    whole = frame_level(level_key, 1.0) * token_noise(noise_key)
    return jnp.clip(whole, -6.0, 6.0).astype(jnp.bfloat16)


def draw_values(key, part):
    key = jax.random.fold_in(key, 11)
    return offset_rows(key, 1.0, 0.5)


def draw_cotangent(key, part):
    key = jax.random.fold_in(key, 23)
    return offset_rows(key, 0.8, 1.0)


def setup_inputs(seed: int = 0) -> dict:
    key_list = jax.random.split(jax.random.key(seed), 5)
    return {
        "queries": draw_queries(jax.random.fold_in(key_list[4], 71), 0),
        "keys": draw_keys(jax.random.fold_in(key_list[4], 71), 0),
        "values": draw_values(jax.random.fold_in(key_list[4], 71), 0),
        "cotangent": draw_cotangent(jax.random.fold_in(key_list[4], 71), 0),
    }


def features(raw_rows):
    return jnp.maximum(raw_rows.astype(jnp.float32), 0.0)


def by_heads(rows):
    return rows.reshape(rows.shape[0], HEADS, HEAD_DIM)


def reference(queries, keys, values, cotangent):
    frames = queries.shape[0]
    tokens = queries.shape[1]
    highest = lax.Precision.HIGHEST

    def block_sums(pair):
        key_feat = features(by_heads(pair[0]))
        value_rows = by_heads(pair[1]).astype(jnp.float32)
        return (jnp.einsum('phi,phj->hij', key_feat, value_rows, precision=highest), jnp.sum(key_feat, axis=0))

    state_blocks, norm_blocks = lax.map(block_sums, (keys, values))
    counts = ((jnp.arange(frames) + 1) * tokens).astype(jnp.float32)
    states = jnp.cumsum(state_blocks, axis=0) / counts[:, None, None, None]
    normals = jnp.cumsum(norm_blocks, axis=0) / counts[:, None, None]

    def query_side(group):
        query_raw, grad_raw, state_now, norm_now, count_now = group
        query_feat = features(by_heads(query_raw))
        grad_rows = by_heads(grad_raw).astype(jnp.float32)
        numer = jnp.einsum('phi,hij->phj', query_feat, state_now, precision=highest)
        denom = jnp.einsum('phi,hi->ph', query_feat, norm_now, precision=highest) + 1.0
        output_rows = numer / denom[..., None]
        grad_numer = grad_rows / denom[..., None]
        grad_denom = -jnp.sum(grad_rows * output_rows, axis=-1) / denom
        grad_feat = jnp.einsum('phj,hij->phi', grad_numer, state_now, precision=highest) + grad_denom[..., None] * norm_now[None]
        grad_query = jnp.where(by_heads(query_raw) > 0, grad_feat, 0.0).astype(jnp.bfloat16)
        state_adj = jnp.einsum('phi,phj->hij', query_feat, grad_numer, precision=highest) / count_now
        norm_adj = jnp.einsum('ph,phi->hi', grad_denom, query_feat, precision=highest) / count_now
        return grad_query.reshape(tokens, HEADS * HEAD_DIM), state_adj, norm_adj

    grad_queries, state_adjs, norm_adjs = lax.map(query_side, (queries, cotangent, states, normals, counts))
    later_states = jnp.flip(jnp.cumsum(jnp.flip(state_adjs, 0), axis=0), 0)
    later_norms = jnp.flip(jnp.cumsum(jnp.flip(norm_adjs, 0), axis=0), 0)

    def key_side(group):
        key_raw, value_raw, state_now, norm_now = group
        key_feat = features(by_heads(key_raw))
        value_rows = by_heads(value_raw).astype(jnp.float32)
        grad_feat = jnp.einsum('phj,hij->phi', value_rows, state_now, precision=highest) + norm_now[None]
        grad_key = jnp.where(by_heads(key_raw) > 0, grad_feat, 0.0).astype(jnp.bfloat16)
        grad_value = jnp.einsum('phi,hij->phj', key_feat, state_now, precision=highest).astype(jnp.bfloat16)
        return grad_key.reshape(tokens, HEADS * HEAD_DIM), grad_value.reshape(tokens, HEADS * HEAD_DIM)

    grad_keys, grad_values = lax.map(key_side, (keys, values, later_states, later_norms))
    return grad_queries, grad_keys, grad_values
```

```python
import jax
import jax.numpy as jnp
from jax import lax
from jax.experimental import pallas as pl
from jax.experimental.pallas import tpu as pltpu
from jax.sharding import PartitionSpec as P

HEAD_DIM = 32
LANES = 128
GROUPS = 9
STEPS = 3
PER_STEP = GROUPS // STEPS
STATE_ROWS = GROUPS * HEAD_DIM
ROWS = 512
FRAME_TOK = 2048

ROW_BY_ROW = (((0,), (0,)), ((), ()))
LANE_BY_LANE = (((1,), (1,)), ((), ()))
PLAIN = (((1,), (0,)), ((), ()))


def dot(lhs, rhs, dims):
    return lax.dot_general(lhs, rhs, dims, preferred_element_type=jnp.float32)


def halves(wide):
    high = wide.astype(jnp.bfloat16)
    low = (wide - high.astype(jnp.float32)).astype(jnp.bfloat16)
    return high, low


def same_head():
    row = lax.broadcasted_iota(jnp.int32, (LANES, LANES), 0)
    lane = lax.broadcasted_iota(jnp.int32, (LANES, LANES), 1)
    return (row // HEAD_DIM) == (lane // HEAD_DIM)


def spread(compact, same):
    return jnp.where(same, jnp.concatenate([compact] * (LANES // HEAD_DIM), axis=0), 0.0)


def gather_heads(full, same):
    full = jnp.where(same, full, 0.0)
    parts = [full[h * HEAD_DIM : (h + 1) * HEAD_DIM] for h in range(LANES // HEAD_DIM)]
    return (parts[0] + parts[1]) + (parts[2] + parts[3])


def block_kernel(key_ref, value_ref, out_ref):
    step = pl.program_id(0)
    same = same_head()

    @pl.when(step == 0)
    def _():
        out_ref[STATE_ROWS:, :] = jnp.zeros((ROWS - STATE_ROWS, LANES), jnp.float32)

    for part in range(PER_STEP):
        group = step * PER_STEP + part
        lanes = slice(part * LANES, (part + 1) * LANES)
        feat = jnp.maximum(key_ref[0, :, lanes], 0)
        full = dot(feat, value_ref[0, :, lanes], ROW_BY_ROW)
        out_ref[pl.ds(group * HEAD_DIM, HEAD_DIM), :] = gather_heads(full, same)
        out_ref[pl.ds(STATE_ROWS + group, 1), :] = jnp.sum(
            feat.astype(jnp.float32), axis=0, keepdims=True
        )


def scan_kernel(backward, sent_ref, out_ref):
    devices = ROWS // 2
    row = lax.broadcasted_iota(jnp.int32, (devices, devices), 0) // 4
    col = lax.broadcasted_iota(jnp.int32, (devices, devices), 1) // 4
    pick = (col >= row) if backward else (col <= row)
    pick = jnp.where(pick, 1.0, 0.0).astype(jnp.bfloat16)
    frame = lax.broadcasted_iota(jnp.int32, (devices, LANES), 0) // 4
    count = ((frame + 1) * FRAME_TOK).astype(jnp.float32)
    for half in range(2):
        rows = pl.ds(half, devices, stride=2)
        terms = sent_ref[rows, :]
        if backward:
            terms = terms / count
        high = terms.astype(jnp.bfloat16)
        rest = terms - high.astype(jnp.float32)
        middle, low = halves(rest)
        total = dot(pick, low, PLAIN) + dot(pick, middle, PLAIN) + dot(pick, high, PLAIN)
        if not backward:
            total = total / count
        out_ref[rows, :] = total


def query_kernel(query_ref, grad_ref, state_ref, out_ref, adj_ref):
    step = pl.program_id(0)
    same = same_head()
    ones = jnp.where(same, 1.0, 0.0).astype(jnp.bfloat16)

    @pl.when(step == 0)
    def _():
        adj_ref[STATE_ROWS:, :] = jnp.zeros((ROWS - STATE_ROWS, LANES), jnp.float32)

    for part in range(PER_STEP):
        group = step * PER_STEP + part
        lanes = slice(part * LANES, (part + 1) * LANES)
        state = spread(state_ref[pl.ds(group * HEAD_DIM, HEAD_DIM), :], same)
        norm = state_ref[pl.ds(STATE_ROWS + group, 1), :]
        state_high, state_low = halves(state)
        norm_high, norm_low = halves(jnp.where(same, norm, 0.0))
        query = query_ref[0, :, lanes]
        grad = grad_ref[0, :, lanes]
        feat = jnp.maximum(query, 0)
        denom = dot(feat, norm_low, LANE_BY_LANE) + dot(feat, norm_high, LANE_BY_LANE) + 1.0
        back = dot(grad, state_low, LANE_BY_LANE) + dot(grad, state_high, LANE_BY_LANE)
        feat_wide = feat.astype(jnp.float32)
        scale = 1.0 / denom
        high, low = halves(feat_wide * back)
        along = dot(low, ones, PLAIN) + dot(high, ones, PLAIN)
        grad_denom = -(along * scale) * scale
        grad_feat = back * scale + grad_denom * norm
        out_ref[0, :, lanes] = jnp.where(
            query.astype(jnp.float32) > 0, grad_feat, 0.0
        ).astype(jnp.bfloat16)
        high, low = halves(grad.astype(jnp.float32) * scale)
        full = dot(feat, low, ROW_BY_ROW) + dot(feat, high, ROW_BY_ROW)
        adj_ref[pl.ds(group * HEAD_DIM, HEAD_DIM), :] = gather_heads(full, same)
        adj_ref[pl.ds(STATE_ROWS + group, 1), :] = jnp.sum(
            grad_denom * feat_wide, axis=0, keepdims=True
        )


def key_kernel(key_ref, value_ref, state_ref, grad_key_ref, grad_value_ref):
    step = pl.program_id(0)
    same = same_head()
    for part in range(PER_STEP):
        group = step * PER_STEP + part
        lanes = slice(part * LANES, (part + 1) * LANES)
        state = spread(state_ref[pl.ds(group * HEAD_DIM, HEAD_DIM), :], same)
        norm = state_ref[pl.ds(STATE_ROWS + group, 1), :]
        high, low = halves(state)
        key = key_ref[0, :, lanes]
        value = value_ref[0, :, lanes]
        feat = jnp.maximum(key, 0)
        grad_feat = dot(value, low, LANE_BY_LANE) + dot(value, high, LANE_BY_LANE) + norm
        grad_key_ref[0, :, lanes] = jnp.where(
            key.astype(jnp.float32) > 0, grad_feat, 0.0
        ).astype(jnp.bfloat16)
        grad_value = dot(feat, low, PLAIN) + dot(feat, high, PLAIN)
        grad_value_ref[0, :, lanes] = grad_value.astype(jnp.bfloat16)


def shards(queries, keys, values, cotangent):
    tokens, channels = queries.shape[1:]
    rows_spec = pl.BlockSpec((1, tokens, PER_STEP * LANES), lambda step: (0, 0, step))
    whole_spec = pl.BlockSpec((ROWS, LANES), lambda step: (0, 0))
    rows_shape = jax.ShapeDtypeStruct((1, tokens, channels), jnp.bfloat16)
    whole_shape = jax.ShapeDtypeStruct((ROWS, LANES), jnp.float32)
    params = pltpu.CompilerParams(vmem_limit_bytes=32 * 1024 * 1024)

    def exchange(whole):
        pieces = whole.reshape(ROWS // 2, 2, LANES)
        pieces = lax.all_to_all(pieces, ("frame", "space"), 0, 0, tiled=True)
        return pieces.reshape(ROWS, LANES)

    def scan(whole, backward):
        return pl.pallas_call(
            lambda sent_ref, out_ref: scan_kernel(backward, sent_ref, out_ref),
            out_shape=whole_shape,
            compiler_params=params,
            name="later" if backward else "earlier",
        )(whole)

    blocks = pl.pallas_call(
        block_kernel,
        grid=(STEPS,),
        in_specs=[rows_spec, rows_spec],
        out_specs=whole_spec,
        out_shape=whole_shape,
        compiler_params=params,
        name="blocks",
    )(keys, values)
    state = exchange(scan(exchange(blocks), False))
    grad_query, adjoint = pl.pallas_call(
        query_kernel,
        grid=(STEPS,),
        in_specs=[rows_spec, rows_spec, whole_spec],
        out_specs=(rows_spec, whole_spec),
        out_shape=(rows_shape, whole_shape),
        compiler_params=params,
        name="queries",
    )(queries, cotangent, state)
    later = exchange(scan(exchange(adjoint), True))
    grad_key, grad_value = pl.pallas_call(
        key_kernel,
        grid=(STEPS,),
        in_specs=[rows_spec, rows_spec, whole_spec],
        out_specs=(rows_spec, rows_spec),
        out_shape=(rows_shape, rows_shape),
        compiler_params=params,
        name="keys",
    )(keys, values, later)
    return (grad_query, grad_key, grad_value)


def solution(mesh):
    placed = P("frame", "space", None)
    return jax.shard_map(
        shards,
        mesh=mesh,
        in_specs=(placed,) * 4,
        out_specs=(placed,) * 3,
        check_vma=False,
    )
```

```python
import jax
import jax.numpy as jnp
from jax import lax
from jax.experimental import pallas as pl
from jax.experimental.pallas import tpu as pltpu
from jax.sharding import Mesh
from jax.sharding import PartitionSpec as P

HEAD_DIM = 32
LANES = 128
GROUPS = 9
STEPS = 3
PER_STEP = GROUPS // STEPS
STATE_ROWS = GROUPS * HEAD_DIM
X, Z, CORES, SPACE = 4, 8, 2, 4
CHUNK = 40
ROWS = CORES * SPACE * CHUNK
FRAME_TOK = 2048

ROW_BY_ROW = (((0,), (0,)), ((), ()))
LANE_BY_LANE = (((1,), (1,)), ((), ()))
PLAIN = (((1,), (0,)), ((), ()))


def dot(lhs, rhs, dims):
    return lax.dot_general(lhs, rhs, dims, preferred_element_type=jnp.float32)


def halves(wide):
    high = wide.astype(jnp.bfloat16)
    low = (wide - high.astype(jnp.float32)).astype(jnp.bfloat16)
    return high, low


def same_head():
    row = lax.broadcasted_iota(jnp.int32, (LANES, LANES), 0)
    lane = lax.broadcasted_iota(jnp.int32, (LANES, LANES), 1)
    return (row // HEAD_DIM) == (lane // HEAD_DIM)


def spread(compact, same):
    return jnp.where(same, jnp.concatenate([compact] * (LANES // HEAD_DIM), axis=0), 0.0)


def gather_heads(full, same):
    full = jnp.where(same, full, 0.0)
    parts = [full[h * HEAD_DIM : (h + 1) * HEAD_DIM] for h in range(LANES // HEAD_DIM)]
    return (parts[0] + parts[1]) + (parts[2] + parts[3])


def block_kernel(key_ref, value_ref, out_ref):
    step = pl.program_id(0)
    same = same_head()

    @pl.when(step == 0)
    def _():
        out_ref[STATE_ROWS:, :] = jnp.zeros((ROWS - STATE_ROWS, LANES), jnp.float32)

    for part in range(PER_STEP):
        group = step * PER_STEP + part
        lanes = slice(part * LANES, (part + 1) * LANES)
        feat = jnp.maximum(key_ref[0, :, lanes], 0)
        full = dot(feat, value_ref[0, :, lanes], ROW_BY_ROW)
        out_ref[pl.ds(group * HEAD_DIM, HEAD_DIM), :] = gather_heads(full, same)
        out_ref[pl.ds(STATE_ROWS + group, 1), :] = jnp.sum(
            feat.astype(jnp.float32), axis=0, keepdims=True
        )


def wrapped(position, shift, size):
    return (position + shift + size) % size


def counted(keep, term):
    return jnp.where(keep, term, 0.0)


def precedes(backward, other, mine):
    return (other > mine) if backward else (other < mine)


def chip_kernel(backward, pieces_ref, edge_ref, both_ref):
    def core(number):
        base = number * SPACE * CHUNK
        parts = [pieces_ref[base + s * CHUNK : base + (s + 1) * CHUNK, :] for s in range(SPACE)]
        return (parts[0] + parts[1]) + (parts[2] + parts[3])

    first, second = core(0), core(1)
    edge_ref[...] = second if backward else first
    both_ref[...] = first + second


def window_kernel(backward, mine_ref, below_ref, above_ref, up_ref, down_ref):
    z = lax.axis_index("z")
    window = ((-1, below_ref[...]), (0, mine_ref[...]), (1, above_ref[...]))
    for out_ref, shift, members in ((up_ref, 3, window), (down_ref, -3, window[:2])):
        target = wrapped(z, shift, Z)
        masked = whole = None
        for offset, term in members:
            kept = counted(precedes(backward, wrapped(z, offset, Z), target), term)
            masked = kept if masked is None else masked + kept
            whole = term if whole is None else whole + term
        out_ref[:CHUNK, :] = masked
        out_ref[CHUNK:, :] = whole


def line_kernel(backward, mine_ref, below_ref, above_ref, lower_ref, upper_ref, masked_ref, whole_ref):
    z = lax.axis_index("z")
    below, above = below_ref[...], above_ref[...]
    near = counted(precedes(backward, wrapped(z, -1, Z), z), below) + counted(
        precedes(backward, wrapped(z, 1, Z), z), above
    )
    masked_ref[...] = near + (lower_ref[:CHUNK, :] + upper_ref[:CHUNK, :])
    whole_ref[...] = (below + mine_ref[...] + above) + (lower_ref[CHUNK:, :] + upper_ref[CHUNK:, :])


def frame_kernel(backward, line_ref, edge_ref, both_ref, *refs):
    x, z = lax.axis_index("x"), lax.axis_index("z")
    out_ref = refs[-1]
    total = line_ref[...]
    for shift, ref in enumerate(refs[:-1], 1):
        total = total + counted(precedes(backward, wrapped(x, -shift, X), x), ref[...])
    edge, both = total + edge_ref[...], total + both_ref[...]
    frames = (both, edge) if backward else (edge, both)
    for core, frame in enumerate(frames):
        if not backward:
            count = ((x * Z + z) * 2 + core + 1) * FRAME_TOK
            frame = frame / count.astype(jnp.float32)
        for s in range(SPACE):
            base = (core * SPACE + s) * CHUNK
            out_ref[base : base + CHUNK, :] = frame


def query_kernel(query_ref, grad_ref, state_ref, out_ref, adj_ref):
    step = pl.program_id(0)
    same = same_head()
    ones = jnp.where(same, 1.0, 0.0).astype(jnp.bfloat16)
    frame = (lax.axis_index("x") * Z + lax.axis_index("z")) * CORES + lax.axis_index("c")
    count = ((frame + 1) * FRAME_TOK).astype(jnp.float32)

    @pl.when(step == 0)
    def _():
        adj_ref[STATE_ROWS:, :] = jnp.zeros((ROWS - STATE_ROWS, LANES), jnp.float32)

    for part in range(PER_STEP):
        group = step * PER_STEP + part
        lanes = slice(part * LANES, (part + 1) * LANES)
        state = spread(state_ref[pl.ds(group * HEAD_DIM, HEAD_DIM), :], same)
        norm = state_ref[pl.ds(STATE_ROWS + group, 1), :]
        state_high, state_low = halves(state)
        norm_high, norm_low = halves(jnp.where(same, norm, 0.0))
        query = query_ref[0, :, lanes]
        grad = grad_ref[0, :, lanes]
        feat = jnp.maximum(query, 0)
        denom = dot(feat, norm_low, LANE_BY_LANE) + dot(feat, norm_high, LANE_BY_LANE) + 1.0
        back = dot(grad, state_low, LANE_BY_LANE) + dot(grad, state_high, LANE_BY_LANE)
        feat_wide = feat.astype(jnp.float32)
        scale = 1.0 / denom
        high, low = halves(feat_wide * back)
        along = dot(low, ones, PLAIN) + dot(high, ones, PLAIN)
        grad_denom = -(along * scale) * scale
        grad_feat = back * scale + grad_denom * norm
        out_ref[0, :, lanes] = jnp.where(
            query.astype(jnp.float32) > 0, grad_feat, 0.0
        ).astype(jnp.bfloat16)
        high, low = halves(grad.astype(jnp.float32) * scale)
        full = dot(feat, low, ROW_BY_ROW) + dot(feat, high, ROW_BY_ROW)
        adj_ref[pl.ds(group * HEAD_DIM, HEAD_DIM), :] = gather_heads(full, same) / count
        adj_ref[pl.ds(STATE_ROWS + group, 1), :] = (
            jnp.sum(grad_denom * feat_wide, axis=0, keepdims=True) / count
        )


def key_kernel(key_ref, value_ref, state_ref, grad_key_ref, grad_value_ref):
    step = pl.program_id(0)
    same = same_head()
    for part in range(PER_STEP):
        group = step * PER_STEP + part
        lanes = slice(part * LANES, (part + 1) * LANES)
        state = spread(state_ref[pl.ds(group * HEAD_DIM, HEAD_DIM), :], same)
        norm = state_ref[pl.ds(STATE_ROWS + group, 1), :]
        high, low = halves(state)
        key = key_ref[0, :, lanes]
        value = value_ref[0, :, lanes]
        feat = jnp.maximum(key, 0)
        grad_feat = dot(value, low, LANE_BY_LANE) + dot(value, high, LANE_BY_LANE) + norm
        grad_key_ref[0, :, lanes] = jnp.where(
            key.astype(jnp.float32) > 0, grad_feat, 0.0
        ).astype(jnp.bfloat16)
        grad_value = dot(feat, low, PLAIN) + dot(feat, high, PLAIN)
        grad_value_ref[0, :, lanes] = grad_value.astype(jnp.bfloat16)


def shards(queries, keys, values, cotangent):
    tokens, channels = queries.shape[1:]
    rows_spec = pl.BlockSpec((1, tokens, PER_STEP * LANES), lambda step: (0, 0, step))
    whole_spec = pl.BlockSpec((ROWS, LANES), lambda step: (0, 0))
    rows_shape = jax.ShapeDtypeStruct((1, tokens, channels), jnp.bfloat16)
    whole_shape = jax.ShapeDtypeStruct((ROWS, LANES), jnp.float32)
    params = pltpu.CompilerParams(vmem_limit_bytes=32 * 1024 * 1024)

    def small(kernel, backward, name, shapes, *args):
        shapes = tuple(jax.ShapeDtypeStruct((rows, LANES), jnp.float32) for rows in shapes)
        return pl.pallas_call(
            lambda *refs: kernel(backward, *refs),
            out_shape=shapes,
            compiler_params=params,
            name=name + ("_later" if backward else "_earlier"),
        )(*args)

    def exchange(whole):
        pieces = whole.reshape(CORES * SPACE, CHUNK, LANES)
        pieces = lax.all_to_all(pieces, ("c", "space"), 0, 0, tiled=True)
        return pieces.reshape(ROWS, LANES)

    def shift(value, axis, size, by):
        return lax.ppermute(value, axis, [(i, (i + by) % size) for i in range(size)])

    def scan(whole, backward):
        edge, both = small(chip_kernel, backward, "chip", (CHUNK, CHUNK), exchange(whole))
        below, above = (shift(both, "z", Z, by) for by in (1, -1))
        up, down = small(
            window_kernel, backward, "window", (2 * CHUNK, 2 * CHUNK), both, below, above
        )
        lower, upper = shift(up, "z", Z, 3), shift(down, "z", Z, -3)
        masked, total = small(
            line_kernel, backward, "line", (CHUNK, CHUNK), both, below, above, lower, upper
        )
        others = [shift(total, "x", X, by) for by in (1, 2, 3)]
        (frames,) = small(frame_kernel, backward, "frame", (ROWS,), masked, edge, both, *others)
        return exchange(frames)

    blocks = pl.pallas_call(
        block_kernel,
        grid=(STEPS,),
        in_specs=[rows_spec, rows_spec],
        out_specs=whole_spec,
        out_shape=whole_shape,
        compiler_params=params,
        name="blocks",
    )(keys, values)
    state = scan(blocks, False)
    grad_query, adjoint = pl.pallas_call(
        query_kernel,
        grid=(STEPS,),
        in_specs=[rows_spec, rows_spec, whole_spec],
        out_specs=(rows_spec, whole_spec),
        out_shape=(rows_shape, whole_shape),
        compiler_params=params,
        name="queries",
    )(queries, cotangent, state)
    later = scan(adjoint, True)
    grad_key, grad_value = pl.pallas_call(
        key_kernel,
        grid=(STEPS,),
        in_specs=[rows_spec, rows_spec, whole_spec],
        out_specs=(rows_spec, rows_spec),
        out_shape=(rows_shape, rows_shape),
        compiler_params=params,
        name="keys",
    )(keys, values, later)
    return (grad_query, grad_key, grad_value)


def solution(mesh):
    split = Mesh(mesh.devices.reshape(X, Z, CORES, SPACE), ("x", "z", "c", "space"))
    placed = P(("x", "z", "c"), "space", None)
    return jax.shard_map(
        shards,
        mesh=split,
        in_specs=(placed,) * 4,
        out_specs=(placed,) * 3,
        check_vma=False,
    )
```

```python
import jax
import jax.numpy as jnp
from jax import lax
from jax.experimental import pallas as pl
from jax.experimental.pallas import tpu as pltpu
from jax.sharding import Mesh
from jax.sharding import PartitionSpec as P

HEAD_DIM = 32
LANES = 128
GROUPS = 9
STEPS = 3
PER_STEP = GROUPS // STEPS
STATE_ROWS = GROUPS * HEAD_DIM
X, Z, CORES, SPACE = 4, 8, 2, 4
CHUNK = 10
PLANE = X * CHUNK
ROWS = X * CORES * SPACE * CHUNK
FRAME_TOK = 2048

ROW_BY_ROW = (((0,), (0,)), ((), ()))
LANE_BY_LANE = (((1,), (1,)), ((), ()))
PLAIN = (((1,), (0,)), ((), ()))


def dot(lhs, rhs, dims):
    return lax.dot_general(lhs, rhs, dims, preferred_element_type=jnp.float32)


def halves(wide):
    high = wide.astype(jnp.bfloat16)
    low = (wide - high.astype(jnp.float32)).astype(jnp.bfloat16)
    return high, low


def same_head():
    row = lax.broadcasted_iota(jnp.int32, (LANES, LANES), 0)
    lane = lax.broadcasted_iota(jnp.int32, (LANES, LANES), 1)
    return (row // HEAD_DIM) == (lane // HEAD_DIM)


def spread(compact, same):
    return jnp.where(same, jnp.concatenate([compact] * (LANES // HEAD_DIM), axis=0), 0.0)


def gather_heads(full, same):
    full = jnp.where(same, full, 0.0)
    parts = [full[h * HEAD_DIM : (h + 1) * HEAD_DIM] for h in range(LANES // HEAD_DIM)]
    return (parts[0] + parts[1]) + (parts[2] + parts[3])


def block_kernel(key_ref, value_ref, out_ref):
    step = pl.program_id(0)
    same = same_head()

    @pl.when(step == 0)
    def _():
        out_ref[STATE_ROWS:, :] = jnp.zeros((ROWS - STATE_ROWS, LANES), jnp.float32)

    for part in range(PER_STEP):
        group = step * PER_STEP + part
        lanes = slice(part * LANES, (part + 1) * LANES)
        feat = jnp.maximum(key_ref[0, :, lanes], 0)
        full = dot(feat, value_ref[0, :, lanes], ROW_BY_ROW)
        out_ref[pl.ds(group * HEAD_DIM, HEAD_DIM), :] = gather_heads(full, same)
        out_ref[pl.ds(STATE_ROWS + group, 1), :] = jnp.sum(
            feat.astype(jnp.float32), axis=0, keepdims=True
        )


def rows_of(x, core, space=0):
    base = ((x * CORES + core) * SPACE + space) * CHUNK
    return slice(base, base + CHUNK)


def plane_kernel(backward, pieces_ref, out_ref, edge_ref, both_ref, ahead_ref):
    z = lax.axis_index("z")
    total = jnp.zeros((CHUNK, LANES), jnp.float32)
    for x in reversed(range(X)) if backward else range(X):
        cores = []
        for core in range(CORES):
            parts = [pieces_ref[rows_of(x, core, s), :] for s in range(SPACE)]
            cores.append((parts[0] + parts[1]) + (parts[2] + parts[3]))
        both = cores[0] + cores[1]
        rows = slice(x * CHUNK, (x + 1) * CHUNK)
        edge_ref[rows, :] = cores[1] if backward else cores[0]
        both_ref[rows, :] = both
        ahead_ref[rows, :] = total
        total = total + both
    ahead, both = ahead_ref[...], both_ref[...]
    for target in range(Z):
        comes = (z > target) if backward else (z < target)
        out_ref[target * PLANE : (target + 1) * PLANE, :] = ahead + jnp.where(comes, both, 0.0)


def frame_kernel(backward, lines_ref, edge_ref, both_ref, out_ref, total_ref):
    z = lax.axis_index("z")
    lines = [lines_ref[i * PLANE : (i + 1) * PLANE, :] for i in range(Z)]
    while len(lines) > 1:
        lines = [first + second for first, second in zip(lines[::2], lines[1::2])]
    for core in range(CORES):
        near = both_ref if (core == 0) == backward else edge_ref
        total_ref[...] = lines[0] + near[...]
        for x in range(X):
            frame = total_ref[x * CHUNK : (x + 1) * CHUNK, :]
            if not backward:
                count = ((x * Z + z) * CORES + core + 1) * FRAME_TOK
                frame = frame / count.astype(jnp.float32)
            for space in range(SPACE):
                out_ref[rows_of(x, core, space), :] = frame


def query_kernel(query_ref, grad_ref, state_ref, out_ref, adj_ref):
    step = pl.program_id(0)
    same = same_head()
    ones = jnp.where(same, 1.0, 0.0).astype(jnp.bfloat16)
    frame = (lax.axis_index("x") * Z + lax.axis_index("z")) * CORES + lax.axis_index("c")
    count = ((frame + 1) * FRAME_TOK).astype(jnp.float32)

    @pl.when(step == 0)
    def _():
        adj_ref[STATE_ROWS:, :] = jnp.zeros((ROWS - STATE_ROWS, LANES), jnp.float32)

    for part in range(PER_STEP):
        group = step * PER_STEP + part
        lanes = slice(part * LANES, (part + 1) * LANES)
        state = spread(state_ref[pl.ds(group * HEAD_DIM, HEAD_DIM), :], same)
        norm = state_ref[pl.ds(STATE_ROWS + group, 1), :]
        state_high, state_low = halves(state)
        norm_high, norm_low = halves(jnp.where(same, norm, 0.0))
        query = query_ref[0, :, lanes]
        grad = grad_ref[0, :, lanes]
        feat = jnp.maximum(query, 0)
        denom = dot(feat, norm_low, LANE_BY_LANE) + dot(feat, norm_high, LANE_BY_LANE) + 1.0
        back = dot(grad, state_low, LANE_BY_LANE) + dot(grad, state_high, LANE_BY_LANE)
        feat_wide = feat.astype(jnp.float32)
        scale = 1.0 / denom
        high, low = halves(feat_wide * back)
        along = dot(low, ones, PLAIN) + dot(high, ones, PLAIN)
        grad_denom = -(along * scale) * scale
        grad_feat = back * scale + grad_denom * norm
        out_ref[0, :, lanes] = jnp.where(
            query.astype(jnp.float32) > 0, grad_feat, 0.0
        ).astype(jnp.bfloat16)
        high, low = halves(grad.astype(jnp.float32) * scale)
        full = dot(feat, low, ROW_BY_ROW) + dot(feat, high, ROW_BY_ROW)
        adj_ref[pl.ds(group * HEAD_DIM, HEAD_DIM), :] = gather_heads(full, same) / count
        adj_ref[pl.ds(STATE_ROWS + group, 1), :] = (
            jnp.sum(grad_denom * feat_wide, axis=0, keepdims=True) / count
        )


def key_kernel(key_ref, value_ref, state_ref, grad_key_ref, grad_value_ref):
    step = pl.program_id(0)
    same = same_head()
    for part in range(PER_STEP):
        group = step * PER_STEP + part
        lanes = slice(part * LANES, (part + 1) * LANES)
        state = spread(state_ref[pl.ds(group * HEAD_DIM, HEAD_DIM), :], same)
        norm = state_ref[pl.ds(STATE_ROWS + group, 1), :]
        high, low = halves(state)
        key = key_ref[0, :, lanes]
        value = value_ref[0, :, lanes]
        feat = jnp.maximum(key, 0)
        grad_feat = dot(value, low, LANE_BY_LANE) + dot(value, high, LANE_BY_LANE) + norm
        grad_key_ref[0, :, lanes] = jnp.where(
            key.astype(jnp.float32) > 0, grad_feat, 0.0
        ).astype(jnp.bfloat16)
        grad_value = dot(feat, low, PLAIN) + dot(feat, high, PLAIN)
        grad_value_ref[0, :, lanes] = grad_value.astype(jnp.bfloat16)


def shards(queries, keys, values, cotangent):
    tokens, channels = queries.shape[1:]
    rows_spec = pl.BlockSpec((1, tokens, PER_STEP * LANES), lambda step: (0, 0, step))
    whole_spec = pl.BlockSpec((ROWS, LANES), lambda step: (0, 0))
    rows_shape = jax.ShapeDtypeStruct((1, tokens, channels), jnp.bfloat16)
    whole_shape = jax.ShapeDtypeStruct((ROWS, LANES), jnp.float32)
    params = pltpu.CompilerParams(vmem_limit_bytes=32 * 1024 * 1024)

    plane_shape = jax.ShapeDtypeStruct((PLANE, LANES), jnp.float32)

    def small(kernel, backward, name, shapes, *args):
        return pl.pallas_call(
            lambda *refs: kernel(backward, *refs),
            out_shape=shapes,
            scratch_shapes=[pltpu.VMEM((PLANE, LANES), jnp.float32)],
            compiler_params=params,
            name=name + ("_later" if backward else "_earlier"),
        )(*args)

    def exchange(whole, axes, peers):
        pieces = whole.reshape(peers, ROWS // peers // 2, 2, LANES)
        return lax.all_to_all(pieces, axes, 0, 0, tiled=True).reshape(ROWS, LANES)

    def scan(whole, backward):
        plane = ("x", "c", "space")
        pieces = exchange(whole, plane, X * CORES * SPACE)
        shapes = (whole_shape, plane_shape, plane_shape)
        lines, edge, both = small(plane_kernel, backward, "plane", shapes, pieces)
        lines = exchange(lines, "z", Z)
        frames = small(frame_kernel, backward, "frame", whole_shape, lines, edge, both)
        return exchange(frames, plane, X * CORES * SPACE)

    blocks = pl.pallas_call(
        block_kernel,
        grid=(STEPS,),
        in_specs=[rows_spec, rows_spec],
        out_specs=whole_spec,
        out_shape=whole_shape,
        compiler_params=params,
        name="blocks",
    )(keys, values)
    state = scan(blocks, False)
    grad_query, adjoint = pl.pallas_call(
        query_kernel,
        grid=(STEPS,),
        in_specs=[rows_spec, rows_spec, whole_spec],
        out_specs=(rows_spec, whole_spec),
        out_shape=(rows_shape, whole_shape),
        compiler_params=params,
        name="queries",
    )(queries, cotangent, state)
    later = scan(adjoint, True)
    grad_key, grad_value = pl.pallas_call(
        key_kernel,
        grid=(STEPS,),
        in_specs=[rows_spec, rows_spec, whole_spec],
        out_specs=(rows_spec, rows_spec),
        out_shape=(rows_shape, rows_shape),
        compiler_params=params,
        name="keys",
    )(keys, values, later)
    return (grad_query, grad_key, grad_value)


def solution(mesh):
    split = Mesh(mesh.devices.reshape(X, Z, CORES, SPACE), ("x", "z", "c", "space"))
    placed = P(("x", "z", "c"), "space", None)
    return jax.shard_map(
        shards,
        mesh=split,
        in_specs=(placed,) * 4,
        out_specs=(placed,) * 3,
        check_vma=False,
    )
```

```python
import jax
import jax.numpy as jnp
from jax import lax
from jax.experimental import pallas as pl
from jax.experimental.pallas import tpu as pltpu
from jax.sharding import Mesh
from jax.sharding import PartitionSpec as P

HEAD_DIM = 32
LANES = 128
GROUPS = 9
STATE_ROWS = GROUPS * HEAD_DIM
X, Z, CORES, SPACE = 4, 8, 2, 4
CHUNK = 10
PLANE = X * CHUNK
ROWS = X * CORES * SPACE * CHUNK
FRAME_TOK = 2048
BYTES = 1 << 20

ROW_BY_ROW = (((0,), (0,)), ((), ()))
LANE_BY_LANE = (((1,), (1,)), ((), ()))
PLAIN = (((1,), (0,)), ((), ()))


def dot(lhs, rhs, dims):
    return lax.dot_general(lhs, rhs, dims, preferred_element_type=jnp.float32)


def halves(wide):
    high = wide.astype(jnp.bfloat16)
    low = (wide - high.astype(jnp.float32)).astype(jnp.bfloat16)
    return high, low


def same_head():
    row = lax.broadcasted_iota(jnp.int32, (LANES, LANES), 0)
    lane = lax.broadcasted_iota(jnp.int32, (LANES, LANES), 1)
    return (row // HEAD_DIM) == (lane // HEAD_DIM)


def spread(compact, same):
    return jnp.where(same, jnp.concatenate([compact] * (LANES // HEAD_DIM), axis=0), 0.0)


def gather_heads(full, same):
    full = jnp.where(same, full, 0.0)
    parts = [full[h * HEAD_DIM : (h + 1) * HEAD_DIM] for h in range(LANES // HEAD_DIM)]
    return (parts[0] + parts[1]) + (parts[2] + parts[3])


def twice(narrow):
    return jnp.concatenate([narrow, narrow], axis=1)


def lanes_of(group):
    return slice(group * LANES, (group + 1) * LANES)


def state_of(group):
    return slice(group * HEAD_DIM, (group + 1) * HEAD_DIM)


def norm_of(group):
    return slice(STATE_ROWS + group, STATE_ROWS + group + 1)


def clear_tail(ref):
    ref[STATE_ROWS:, :] = jnp.zeros((ROWS - STATE_ROWS, LANES), jnp.float32)


def block_kernel(key_hbm, value_hbm, out_ref, key_ref, value_ref, sem):
    same = same_head()
    half = key_ref.shape[1] // 2
    pieces = [slice(0, half), slice(half, 2 * half)]
    copies = []
    for i, rows in enumerate(pieces):
        for j, (source, target) in enumerate(((key_hbm, key_ref), (value_hbm, value_ref))):
            copy = pltpu.make_async_copy(source.at[:, rows], target.at[:, rows], sem.at[2 * i + j])
            copy.start()
            copies.append(copy)
    clear_tail(out_ref)
    for i, rows in enumerate(pieces):
        copies[2 * i].wait()
        copies[2 * i + 1].wait()
        for group in range(GROUPS):
            feat = jnp.maximum(key_ref[0, rows, lanes_of(group)], 0)
            full = dot(feat, value_ref[0, rows, lanes_of(group)], ROW_BY_ROW)
            state = gather_heads(full, same)
            norm = jnp.sum(feat.astype(jnp.float32), axis=0, keepdims=True)
            if i:
                state = state + out_ref[state_of(group), :]
                norm = norm + out_ref[norm_of(group), :]
            out_ref[state_of(group), :] = state
            out_ref[norm_of(group), :] = norm


def rows_of(x, core, space=0):
    base = ((x * CORES + core) * SPACE + space) * CHUNK
    return slice(base, base + CHUNK)


def plane_kernel(backward, pieces_ref, out_ref, edge_ref, both_ref, ahead_ref):
    z = lax.axis_index("z")
    total = jnp.zeros((CHUNK, LANES), jnp.float32)
    for x in reversed(range(X)) if backward else range(X):
        cores = []
        for core in range(CORES):
            parts = [pieces_ref[rows_of(x, core, s), :] for s in range(SPACE)]
            cores.append((parts[0] + parts[1]) + (parts[2] + parts[3]))
        both = cores[0] + cores[1]
        rows = slice(x * CHUNK, (x + 1) * CHUNK)
        edge_ref[rows, :] = cores[1] if backward else cores[0]
        both_ref[rows, :] = both
        ahead_ref[rows, :] = total
        total = total + both
    ahead, both = ahead_ref[...], both_ref[...]
    for target in range(Z):
        comes = (z > target) if backward else (z < target)
        out_ref[target * PLANE : (target + 1) * PLANE, :] = ahead + jnp.where(comes, both, 0.0)


def frame_kernel(backward, lines_ref, edge_ref, both_ref, out_ref, total_ref):
    z = lax.axis_index("z")
    lines = [lines_ref[i * PLANE : (i + 1) * PLANE, :] for i in range(Z)]
    while len(lines) > 1:
        lines = [first + second for first, second in zip(lines[::2], lines[1::2])]
    for core in range(CORES):
        near = both_ref if (core == 0) == backward else edge_ref
        total_ref[...] = lines[0] + near[...]
        for x in range(X):
            frame = total_ref[x * CHUNK : (x + 1) * CHUNK, :]
            if not backward:
                count = ((x * Z + z) * CORES + core + 1) * FRAME_TOK
                frame = frame / count.astype(jnp.float32)
            for space in range(SPACE):
                out_ref[rows_of(x, core, space), :] = frame


def query_kernel(query_ref, grad_ref, state_ref, out_ref, adj_ref):
    same = same_head()
    ones = jnp.where(same, 1.0, 0.0).astype(jnp.bfloat16)
    ones = jnp.concatenate([ones, ones], axis=0)
    frame = (lax.axis_index("x") * Z + lax.axis_index("z")) * CORES + lax.axis_index("c")
    count = ((frame + 1) * FRAME_TOK).astype(jnp.float32)
    clear_tail(adj_ref)

    def project(group):
        feat = jnp.maximum(query_ref[0, :, lanes_of(group)], 0)
        grad = grad_ref[0, :, lanes_of(group)]
        state = spread(state_ref[state_of(group), :], same)
        norm = jnp.where(same, state_ref[norm_of(group), :], 0.0)
        denom = dot(twice(feat), jnp.concatenate(halves(norm), axis=1), LANE_BY_LANE) + 1.0
        back = dot(twice(grad), jnp.concatenate(halves(state), axis=1), LANE_BY_LANE)
        return denom, back

    def finish(group, denom, back):
        feat = jnp.maximum(query_ref[0, :, lanes_of(group)], 0)
        grad = grad_ref[0, :, lanes_of(group)].astype(jnp.float32)
        wide = feat.astype(jnp.float32)
        scale = 1.0 / denom
        along = dot(jnp.concatenate(halves(wide * back), axis=1), ones, PLAIN)
        pull = along * scale
        grad_feat = scale * (back - pull * state_ref[norm_of(group), :])
        out_ref[0, :, lanes_of(group)] = jnp.where(wide > 0, grad_feat, 0.0).astype(jnp.bfloat16)
        full = dot(feat, jnp.concatenate(halves(grad * scale), axis=1), ROW_BY_ROW)
        full = full[:, :LANES] + full[:, LANES:]
        adj_ref[state_of(group), :] = gather_heads(full, same) / count
        norm = jnp.sum(pull * scale * wide, axis=0, keepdims=True)
        adj_ref[norm_of(group), :] = -norm / count

    ahead = project(0)
    for group in range(GROUPS):
        ready = ahead
        if group + 1 < GROUPS:
            ahead = project(group + 1)
        finish(group, *ready)


def key_kernel(key_ref, value_ref, state_ref, grad_key_out, grad_value_out, grad_key, grad_value, sem):
    same = same_head()
    copies = []
    for group in range(GROUPS):
        lanes = lanes_of(group)
        high, low = halves(spread(state_ref[state_of(group), :], same))
        key = key_ref[0, :, lanes]
        feat = jnp.maximum(key, 0)
        grad_feat = dot(
            twice(value_ref[0, :, lanes]), jnp.concatenate([high, low], axis=1), LANE_BY_LANE
        )
        grad_feat = grad_feat + state_ref[norm_of(group), :]
        grad_key[0, :, lanes] = jnp.where(key.astype(jnp.float32) > 0, grad_feat, 0.0).astype(
            jnp.bfloat16
        )
        grad_value[0, :, lanes] = dot(
            twice(feat), jnp.concatenate([high, low], axis=0), PLAIN
        ).astype(jnp.bfloat16)
        pairs = ((grad_key, grad_key_out), (grad_value, grad_value_out))
        for j, (source, target) in enumerate(pairs):
            copy = pltpu.make_async_copy(
                source.at[:, :, lanes], target.at[:, :, lanes], sem.at[2 * group + j]
            )
            copy.start()
            copies.append(copy)
    for copy in copies:
        copy.wait()


def shards(queries, keys, values, cotangent):
    vmem = pl.BlockSpec(memory_space=pltpu.VMEM)
    hbm = pl.BlockSpec(memory_space=pl.ANY)
    rows_shape = jax.ShapeDtypeStruct(queries.shape, jnp.bfloat16)
    rows_scratch = pltpu.VMEM(queries.shape, jnp.bfloat16)
    whole_shape = jax.ShapeDtypeStruct((ROWS, LANES), jnp.float32)
    params = pltpu.CompilerParams(vmem_limit_bytes=32 * BYTES)
    plane_shape = jax.ShapeDtypeStruct((PLANE, LANES), jnp.float32)

    def small(kernel, backward, name, shapes, *args):
        return pl.pallas_call(
            lambda *refs: kernel(backward, *refs),
            out_shape=shapes,
            scratch_shapes=[pltpu.VMEM((PLANE, LANES), jnp.float32)],
            compiler_params=params,
            name=name + ("_later" if backward else "_earlier"),
        )(*args)

    def exchange(whole, axes, peers):
        pieces = whole.reshape(peers, ROWS // peers // 2, 2, LANES)
        return lax.all_to_all(pieces, axes, 0, 0, tiled=True).reshape(ROWS, LANES)

    def scan(whole, backward):
        plane = ("x", "c", "space")
        pieces = exchange(whole, plane, X * CORES * SPACE)
        shapes = (whole_shape, plane_shape, plane_shape)
        lines, edge, both = small(plane_kernel, backward, "plane", shapes, pieces)
        lines = exchange(lines, "z", Z)
        frames = small(frame_kernel, backward, "frame", whole_shape, lines, edge, both)
        return exchange(frames, plane, X * CORES * SPACE)

    blocks = pl.pallas_call(
        block_kernel,
        in_specs=[hbm, hbm],
        out_specs=vmem,
        out_shape=whole_shape,
        scratch_shapes=[rows_scratch, rows_scratch, pltpu.SemaphoreType.DMA((4,))],
        compiler_params=pltpu.CompilerParams(vmem_limit_bytes=60 * BYTES),
        name="blocks",
    )(keys, values)
    state = scan(blocks, False)
    grad_query, adjoint = pl.pallas_call(
        query_kernel,
        in_specs=[vmem] * 3,
        out_specs=(vmem, vmem),
        out_shape=(rows_shape, whole_shape),
        compiler_params=params,
        name="queries",
    )(queries, cotangent, state)
    later = scan(adjoint, True)
    grad_key, grad_value = pl.pallas_call(
        key_kernel,
        in_specs=[vmem] * 3,
        out_specs=(hbm, hbm),
        out_shape=(rows_shape, rows_shape),
        scratch_shapes=[rows_scratch, rows_scratch, pltpu.SemaphoreType.DMA((2 * GROUPS,))],
        compiler_params=params,
        name="keys",
    )(keys, values, later)
    return (grad_query, grad_key, grad_value)


def solution(mesh):
    split = Mesh(mesh.devices.reshape(X, Z, CORES, SPACE), ("x", "z", "c", "space"))
    placed = P(("x", "z", "c"), "space", None)
    return jax.shard_map(
        shards,
        mesh=split,
        in_specs=(placed,) * 4,
        out_specs=(placed,) * 3,
        check_vma=False,
    )
```

```python
import jax
import jax.numpy as jnp
from jax import lax
from jax.experimental import pallas as pl
from jax.experimental.pallas import tpu as pltpu
from jax.sharding import Mesh
from jax.sharding import PartitionSpec as P

HEAD_DIM = 32
LANES = 128
GROUPS = 9
STATE_ROWS = GROUPS * HEAD_DIM
X, Z, CORES, SPACE = 4, 8, 2, 4
CHUNK = 10
PLANE = X * CHUNK
ROWS = X * CORES * SPACE * CHUNK
FRAME_TOK = 2048
ENDS = {3: 0, 7: 4, 8: 8}
BYTES = 1 << 20

ROW_BY_ROW = (((0,), (0,)), ((), ()))
LANE_BY_LANE = (((1,), (1,)), ((), ()))
PLAIN = (((1,), (0,)), ((), ()))


def dot(lhs, rhs, dims):
    return lax.dot_general(lhs, rhs, dims, preferred_element_type=jnp.float32)


def halves(wide):
    high = wide.astype(jnp.bfloat16)
    low = (wide - high.astype(jnp.float32)).astype(jnp.bfloat16)
    return high, low


def same_head():
    row = lax.broadcasted_iota(jnp.int32, (LANES, LANES), 0)
    lane = lax.broadcasted_iota(jnp.int32, (LANES, LANES), 1)
    return (row // HEAD_DIM) == (lane // HEAD_DIM)


def spread(compact, same):
    return jnp.where(same, jnp.concatenate([compact] * (LANES // HEAD_DIM), axis=0), 0.0)


def gather_heads(full, same):
    full = jnp.where(same, full, 0.0)
    parts = [full[h * HEAD_DIM : (h + 1) * HEAD_DIM] for h in range(LANES // HEAD_DIM)]
    return (parts[0] + parts[1]) + (parts[2] + parts[3])


def twice(narrow):
    return jnp.concatenate([narrow, narrow], axis=1)


def lanes_of(group):
    return slice(group * LANES, (group + 1) * LANES)


def pair_of(group):
    return slice(2 * group * LANES, 2 * (group + 1) * LANES)


def state_of(group):
    return slice(group * HEAD_DIM, (group + 1) * HEAD_DIM)


def norm_of(group):
    return slice(STATE_ROWS + group, STATE_ROWS + group + 1)


def clear_tail(ref):
    ref[STATE_ROWS:, :] = jnp.zeros((ROWS - STATE_ROWS, LANES), jnp.float32)


def block_kernel(key_hbm, value_hbm, out_ref, key_ref, value_ref, sem):
    same = same_head()
    half = key_ref.shape[1] // 2
    pieces = [slice(0, half), slice(half, 2 * half)]
    copies = []
    for i, rows in enumerate(pieces):
        for j, (source, target) in enumerate(((key_hbm, key_ref), (value_hbm, value_ref))):
            copy = pltpu.make_async_copy(source.at[:, rows], target.at[:, rows], sem.at[2 * i + j])
            copy.start()
            copies.append(copy)
    clear_tail(out_ref)
    for i, rows in enumerate(pieces):
        copies[2 * i].wait()
        copies[2 * i + 1].wait()
        for group in range(GROUPS):
            feat = jnp.maximum(key_ref[0, rows, lanes_of(group)], 0)
            full = dot(feat, value_ref[0, rows, lanes_of(group)], ROW_BY_ROW)
            state = gather_heads(full, same)
            norm = jnp.sum(feat.astype(jnp.float32), axis=0, keepdims=True)
            if i:
                state = state + out_ref[state_of(group), :]
                norm = norm + out_ref[norm_of(group), :]
            out_ref[state_of(group), :] = state
            out_ref[norm_of(group), :] = norm


def rows_of(x, core, space=0):
    base = ((x * CORES + core) * SPACE + space) * CHUNK
    return slice(base, base + CHUNK)


def plane_kernel(backward, pieces_ref, out_ref, edge_ref, both_ref, ahead_ref):
    z = lax.axis_index("z")
    total = jnp.zeros((CHUNK, LANES), jnp.float32)
    for x in reversed(range(X)) if backward else range(X):
        cores = []
        for core in range(CORES):
            parts = [pieces_ref[rows_of(x, core, s), :] for s in range(SPACE)]
            cores.append((parts[0] + parts[1]) + (parts[2] + parts[3]))
        both = cores[0] + cores[1]
        rows = slice(x * CHUNK, (x + 1) * CHUNK)
        edge_ref[rows, :] = cores[1] if backward else cores[0]
        both_ref[rows, :] = both
        ahead_ref[rows, :] = total
        total = total + both
    ahead, both = ahead_ref[...], both_ref[...]
    for target in range(Z):
        comes = (z > target) if backward else (z < target)
        out_ref[target * PLANE : (target + 1) * PLANE, :] = ahead + jnp.where(comes, both, 0.0)


def frame_kernel(backward, lines_ref, edge_ref, both_ref, out_ref, total_ref):
    z = lax.axis_index("z")
    lines = [lines_ref[i * PLANE : (i + 1) * PLANE, :] for i in range(Z)]
    while len(lines) > 1:
        lines = [first + second for first, second in zip(lines[::2], lines[1::2])]
    for core in range(CORES):
        near = both_ref if (core == 0) == backward else edge_ref
        total_ref[...] = lines[0] + near[...]
        for x in range(X):
            frame = total_ref[x * CHUNK : (x + 1) * CHUNK, :]
            if not backward:
                count = ((x * Z + z) * CORES + core + 1) * FRAME_TOK
                frame = frame / count.astype(jnp.float32)
            for space in range(SPACE):
                out_ref[rows_of(x, core, space), :] = frame


def query_kernel(query_ref, grad_ref, state_ref, out_hbm, adj_ref, out_ref, pair_ref, sem):
    same = same_head()
    ones = jnp.where(same, 1.0, 0.0).astype(jnp.bfloat16)
    ones = jnp.concatenate([ones, ones], axis=0)
    frame = (lax.axis_index("x") * Z + lax.axis_index("z")) * CORES + lax.axis_index("c")
    count = ((frame + 1) * FRAME_TOK).astype(jnp.float32)
    clear_tail(adj_ref)
    copies = []

    def project(group):
        feat = jnp.maximum(query_ref[0, :, lanes_of(group)], 0)
        grad = grad_ref[0, :, lanes_of(group)]
        state = spread(state_ref[state_of(group), :], same)
        norm = jnp.where(same, state_ref[norm_of(group), :], 0.0)
        denom = dot(twice(feat), jnp.concatenate(halves(norm), axis=1), LANE_BY_LANE) + 1.0
        back = dot(twice(grad), jnp.concatenate(halves(state), axis=1), LANE_BY_LANE)
        return denom, back

    def finish(group, denom, back):
        feat = jnp.maximum(query_ref[0, :, lanes_of(group)], 0)
        grad = grad_ref[0, :, lanes_of(group)].astype(jnp.float32)
        wide = feat.astype(jnp.float32)
        scale = 1.0 / denom
        along = dot(jnp.concatenate(halves(wide * back), axis=1), ones, PLAIN)
        pull = along * scale
        grad_feat = scale * (back - pull * state_ref[norm_of(group), :])
        out_ref[0, :, lanes_of(group)] = jnp.where(wide > 0, grad_feat, 0.0).astype(jnp.bfloat16)
        if group in ENDS:
            lanes = slice(ENDS[group] * LANES, (group + 1) * LANES)
            copy = pltpu.make_async_copy(
                out_ref.at[:, :, lanes], out_hbm.at[:, :, lanes], sem.at[len(copies)]
            )
            copy.start()
            copies.append(copy)
        pair_ref[:, pair_of(group)] = jnp.concatenate(halves(grad * scale), axis=1)
        norm = jnp.sum(pull * scale * wide, axis=0, keepdims=True)
        adj_ref[norm_of(group), :] = -norm / count

    ahead = project(0)
    for group in range(GROUPS):
        ready = ahead
        if group + 1 < GROUPS:
            ahead = project(group + 1)
        finish(group, *ready)
    for group in range(GROUPS):
        feat = jnp.maximum(query_ref[0, :, lanes_of(group)], 0)
        full = dot(feat, pair_ref[:, pair_of(group)], ROW_BY_ROW)
        full = full[:, :LANES] + full[:, LANES:]
        adj_ref[state_of(group), :] = gather_heads(full, same) / count
    for copy in copies:
        copy.wait()


def key_kernel(key_ref, value_ref, state_ref, grad_key_out, grad_value_out, grad_key, grad_value, sem):
    same = same_head()
    copies = []
    for group in range(GROUPS):
        lanes = lanes_of(group)
        high, low = halves(spread(state_ref[state_of(group), :], same))
        key = key_ref[0, :, lanes]
        feat = jnp.maximum(key, 0)
        grad_feat = dot(
            twice(value_ref[0, :, lanes]), jnp.concatenate([high, low], axis=1), LANE_BY_LANE
        )
        grad_feat = grad_feat + state_ref[norm_of(group), :]
        grad_key[0, :, lanes] = jnp.where(key.astype(jnp.float32) > 0, grad_feat, 0.0).astype(
            jnp.bfloat16
        )
        grad_value[0, :, lanes] = dot(
            twice(feat), jnp.concatenate([high, low], axis=0), PLAIN
        ).astype(jnp.bfloat16)
        pairs = ((grad_key, grad_key_out), (grad_value, grad_value_out))
        for j, (source, target) in enumerate(pairs):
            copy = pltpu.make_async_copy(
                source.at[:, :, lanes], target.at[:, :, lanes], sem.at[2 * group + j]
            )
            copy.start()
            copies.append(copy)
    for copy in copies:
        copy.wait()


def shards(queries, keys, values, cotangent):
    vmem = pl.BlockSpec(memory_space=pltpu.VMEM)
    hbm = pl.BlockSpec(memory_space=pl.ANY)
    rows_shape = jax.ShapeDtypeStruct(queries.shape, jnp.bfloat16)
    rows_scratch = pltpu.VMEM(queries.shape, jnp.bfloat16)
    whole_shape = jax.ShapeDtypeStruct((ROWS, LANES), jnp.float32)
    params = pltpu.CompilerParams(vmem_limit_bytes=32 * BYTES)
    plane_shape = jax.ShapeDtypeStruct((PLANE, LANES), jnp.float32)

    def small(kernel, backward, name, shapes, *args):
        return pl.pallas_call(
            lambda *refs: kernel(backward, *refs),
            out_shape=shapes,
            scratch_shapes=[pltpu.VMEM((PLANE, LANES), jnp.float32)],
            compiler_params=params,
            name=name + ("_later" if backward else "_earlier"),
        )(*args)

    def exchange(whole, axes, peers):
        pieces = whole.reshape(peers, ROWS // peers // 2, 2, LANES)
        return lax.all_to_all(pieces, axes, 0, 0, tiled=True).reshape(ROWS, LANES)

    def scan(whole, backward):
        plane = ("x", "c", "space")
        pieces = exchange(whole, plane, X * CORES * SPACE)
        shapes = (whole_shape, plane_shape, plane_shape)
        lines, edge, both = small(plane_kernel, backward, "plane", shapes, pieces)
        lines = exchange(lines, "z", Z)
        frames = small(frame_kernel, backward, "frame", whole_shape, lines, edge, both)
        return exchange(frames, plane, X * CORES * SPACE)

    blocks = pl.pallas_call(
        block_kernel,
        in_specs=[hbm, hbm],
        out_specs=vmem,
        out_shape=whole_shape,
        scratch_shapes=[rows_scratch, rows_scratch, pltpu.SemaphoreType.DMA((4,))],
        compiler_params=pltpu.CompilerParams(vmem_limit_bytes=60 * BYTES),
        name="blocks",
    )(keys, values)
    state = scan(blocks, False)
    grad_query, adjoint = pl.pallas_call(
        query_kernel,
        in_specs=[vmem] * 3,
        out_specs=(hbm, vmem),
        out_shape=(rows_shape, whole_shape),
        scratch_shapes=[
            rows_scratch,
            pltpu.VMEM((queries.shape[1], 2 * queries.shape[2]), jnp.bfloat16),
            pltpu.SemaphoreType.DMA((len(ENDS),)),
        ],
        compiler_params=params,
        name="queries",
    )(queries, cotangent, state)
    later = scan(adjoint, True)
    grad_key, grad_value = pl.pallas_call(
        key_kernel,
        in_specs=[vmem] * 3,
        out_specs=(hbm, hbm),
        out_shape=(rows_shape, rows_shape),
        scratch_shapes=[rows_scratch, rows_scratch, pltpu.SemaphoreType.DMA((2 * GROUPS,))],
        compiler_params=params,
        name="keys",
    )(keys, values, later)
    return (grad_query, grad_key, grad_value)


def solution(mesh):
    split = Mesh(mesh.devices.reshape(X, Z, CORES, SPACE), ("x", "z", "c", "space"))
    placed = P(("x", "z", "c"), "space", None)
    return jax.shard_map(
        shards,
        mesh=split,
        in_specs=(placed,) * 4,
        out_specs=(placed,) * 3,
        check_vma=False,
    )
```

```python
import jax
import jax.numpy as jnp
from jax import lax
from jax.experimental import pallas as pl
from jax.experimental.pallas import tpu as pltpu
from jax.sharding import Mesh
from jax.sharding import PartitionSpec as P

HEAD_DIM = 32
LANES = 128
GROUPS = 9
STATE_ROWS = GROUPS * HEAD_DIM
X, Z, CORES, SPACE = 4, 8, 2, 4
CHUNK = 10
PLANE = X * CHUNK
ROWS = X * CORES * SPACE * CHUNK
FRAME_TOK = 2048
ENDS = {3: 0, 7: 4, 8: 8}
BYTES = 1 << 20

ROW_BY_ROW = (((0,), (0,)), ((), ()))
LANE_BY_LANE = (((1,), (1,)), ((), ()))
PLAIN = (((1,), (0,)), ((), ()))


def dot(lhs, rhs, dims):
    return lax.dot_general(lhs, rhs, dims, preferred_element_type=jnp.float32)


def halves(wide):
    high = wide.astype(jnp.bfloat16)
    low = (wide - high.astype(jnp.float32)).astype(jnp.bfloat16)
    return high, low


def same_head():
    row = lax.broadcasted_iota(jnp.int32, (LANES, LANES), 0)
    lane = lax.broadcasted_iota(jnp.int32, (LANES, LANES), 1)
    return (row // HEAD_DIM) == (lane // HEAD_DIM)


def spread(compact, same):
    return jnp.where(same, jnp.concatenate([compact] * (LANES // HEAD_DIM), axis=0), 0.0)


def gather_heads(full, same):
    full = jnp.where(same, full, 0.0)
    parts = [full[h * HEAD_DIM : (h + 1) * HEAD_DIM] for h in range(LANES // HEAD_DIM)]
    return (parts[0] + parts[1]) + (parts[2] + parts[3])


def twice(narrow):
    return jnp.concatenate([narrow, narrow], axis=1)


def lanes_of(group):
    return slice(group * LANES, (group + 1) * LANES)


def pair_of(group):
    return slice(2 * group * LANES, 2 * (group + 1) * LANES)


def state_of(group):
    return slice(group * HEAD_DIM, (group + 1) * HEAD_DIM)


def norm_of(group):
    return slice(STATE_ROWS + group, STATE_ROWS + group + 1)


def clear_tail(ref):
    ref[STATE_ROWS:, :] = jnp.zeros((ROWS - STATE_ROWS, LANES), jnp.float32)


def block_kernel(key_hbm, value_hbm, out_ref, key_ref, value_ref, sem):
    same = same_head()
    half = key_ref.shape[1] // 2
    pieces = [slice(0, half), slice(half, 2 * half)]
    copies = []
    for i, rows in enumerate(pieces):
        for j, (source, target) in enumerate(((key_hbm, key_ref), (value_hbm, value_ref))):
            copy = pltpu.make_async_copy(source.at[:, rows], target.at[:, rows], sem.at[2 * i + j])
            copy.start()
            copies.append(copy)
    clear_tail(out_ref)
    for i, rows in enumerate(pieces):
        copies[2 * i].wait()
        copies[2 * i + 1].wait()
        feats = [jnp.maximum(key_ref[0, rows, lanes_of(group)], 0) for group in range(GROUPS)]
        fulls = [
            dot(feats[group], value_ref[0, rows, lanes_of(group)], ROW_BY_ROW)
            for group in range(GROUPS)
        ]
        for group in range(GROUPS):
            norm = jnp.sum(feats[group].astype(jnp.float32), axis=0, keepdims=True)
            state = gather_heads(fulls[group], same)
            if i:
                state = state + out_ref[state_of(group), :]
                norm = norm + out_ref[norm_of(group), :]
            out_ref[state_of(group), :] = state
            out_ref[norm_of(group), :] = norm


def rows_of(x, core, space=0):
    base = ((x * CORES + core) * SPACE + space) * CHUNK
    return slice(base, base + CHUNK)


def plane_kernel(backward, pieces_ref, out_ref, edge_ref, both_ref, ahead_ref):
    z = lax.axis_index("z")
    total = jnp.zeros((CHUNK, LANES), jnp.float32)
    for x in reversed(range(X)) if backward else range(X):
        cores = []
        for core in range(CORES):
            parts = [pieces_ref[rows_of(x, core, s), :] for s in range(SPACE)]
            cores.append((parts[0] + parts[1]) + (parts[2] + parts[3]))
        both = cores[0] + cores[1]
        rows = slice(x * CHUNK, (x + 1) * CHUNK)
        edge_ref[rows, :] = cores[1] if backward else cores[0]
        both_ref[rows, :] = both
        ahead_ref[rows, :] = total
        total = total + both
    ahead, both = ahead_ref[...], both_ref[...]
    for target in range(Z):
        comes = (z > target) if backward else (z < target)
        out_ref[target * PLANE : (target + 1) * PLANE, :] = ahead + jnp.where(comes, both, 0.0)


def frame_kernel(backward, lines_ref, edge_ref, both_ref, out_ref, total_ref):
    z = lax.axis_index("z")
    lines = [lines_ref[i * PLANE : (i + 1) * PLANE, :] for i in range(Z)]
    while len(lines) > 1:
        lines = [first + second for first, second in zip(lines[::2], lines[1::2])]
    for core in range(CORES):
        near = both_ref if (core == 0) == backward else edge_ref
        total_ref[...] = lines[0] + near[...]
        for x in range(X):
            frame = total_ref[x * CHUNK : (x + 1) * CHUNK, :]
            if not backward:
                count = ((x * Z + z) * CORES + core + 1) * FRAME_TOK
                frame = frame / count.astype(jnp.float32)
            for space in range(SPACE):
                out_ref[rows_of(x, core, space), :] = frame


def query_kernel(query_ref, grad_ref, state_ref, out_hbm, adj_ref, out_ref, pair_ref, sem):
    same = same_head()
    ones = jnp.where(same, 1.0, 0.0).astype(jnp.bfloat16)
    ones = jnp.concatenate([ones, ones], axis=0)
    frame = (lax.axis_index("x") * Z + lax.axis_index("z")) * CORES + lax.axis_index("c")
    count = ((frame + 1) * FRAME_TOK).astype(jnp.float32)
    clear_tail(adj_ref)
    copies = []

    def project(group):
        feat = jnp.maximum(query_ref[0, :, lanes_of(group)], 0)
        grad = grad_ref[0, :, lanes_of(group)]
        state = spread(state_ref[state_of(group), :], same)
        norm = jnp.where(same, state_ref[norm_of(group), :], 0.0)
        denom = dot(twice(feat), jnp.concatenate(halves(norm), axis=1), LANE_BY_LANE) + 1.0
        back = dot(twice(grad), jnp.concatenate(halves(state), axis=1), LANE_BY_LANE)
        return denom, back

    def finish(group, denom, back):
        feat = jnp.maximum(query_ref[0, :, lanes_of(group)], 0)
        grad = grad_ref[0, :, lanes_of(group)].astype(jnp.float32)
        wide = feat.astype(jnp.float32)
        scale = 1.0 / denom
        along = dot(jnp.concatenate(halves(wide * back), axis=1), ones, PLAIN)
        pull = along * scale
        grad_feat = scale * (back - pull * state_ref[norm_of(group), :])
        out_ref[0, :, lanes_of(group)] = jnp.where(wide > 0, grad_feat, 0.0).astype(jnp.bfloat16)
        if group in ENDS:
            lanes = slice(ENDS[group] * LANES, (group + 1) * LANES)
            copy = pltpu.make_async_copy(
                out_ref.at[:, :, lanes], out_hbm.at[:, :, lanes], sem.at[len(copies)]
            )
            copy.start()
            copies.append(copy)
        pair_ref[:, pair_of(group)] = jnp.concatenate(halves(grad * scale), axis=1)
        norm = jnp.sum(pull * scale * wide, axis=0, keepdims=True)
        adj_ref[norm_of(group), :] = -norm / count

    ahead = project(0)
    for group in range(GROUPS):
        ready = ahead
        if group + 1 < GROUPS:
            ahead = project(group + 1)
        finish(group, *ready)
    for group in range(GROUPS):
        feat = jnp.maximum(query_ref[0, :, lanes_of(group)], 0)
        full = dot(feat, pair_ref[:, pair_of(group)], ROW_BY_ROW)
        full = full[:, :LANES] + full[:, LANES:]
        adj_ref[state_of(group), :] = gather_heads(full, same) / count
    for copy in copies:
        copy.wait()


def key_kernel(key_ref, value_ref, state_ref, grad_key_out, grad_value_out, grad_key, grad_value, sem):
    same = same_head()
    copies = []
    for group in range(GROUPS):
        lanes = lanes_of(group)
        high, low = halves(spread(state_ref[state_of(group), :], same))
        key = key_ref[0, :, lanes]
        feat = jnp.maximum(key, 0)
        grad_feat = dot(
            twice(value_ref[0, :, lanes]), jnp.concatenate([high, low], axis=1), LANE_BY_LANE
        )
        grad_feat = grad_feat + state_ref[norm_of(group), :]
        grad_key[0, :, lanes] = jnp.where(key.astype(jnp.float32) > 0, grad_feat, 0.0).astype(
            jnp.bfloat16
        )
        grad_value[0, :, lanes] = dot(
            twice(feat), jnp.concatenate([high, low], axis=0), PLAIN
        ).astype(jnp.bfloat16)
        pairs = ((grad_key, grad_key_out), (grad_value, grad_value_out))
        for j, (source, target) in enumerate(pairs):
            copy = pltpu.make_async_copy(
                source.at[:, :, lanes], target.at[:, :, lanes], sem.at[2 * group + j]
            )
            copy.start()
            copies.append(copy)
    for copy in copies:
        copy.wait()


def shards(queries, keys, values, cotangent):
    vmem = pl.BlockSpec(memory_space=pltpu.VMEM)
    hbm = pl.BlockSpec(memory_space=pl.ANY)
    rows_shape = jax.ShapeDtypeStruct(queries.shape, jnp.bfloat16)
    rows_scratch = pltpu.VMEM(queries.shape, jnp.bfloat16)
    whole_shape = jax.ShapeDtypeStruct((ROWS, LANES), jnp.float32)
    params = pltpu.CompilerParams(vmem_limit_bytes=32 * BYTES)
    plane_shape = jax.ShapeDtypeStruct((PLANE, LANES), jnp.float32)

    def small(kernel, backward, name, shapes, *args):
        return pl.pallas_call(
            lambda *refs: kernel(backward, *refs),
            out_shape=shapes,
            scratch_shapes=[pltpu.VMEM((PLANE, LANES), jnp.float32)],
            compiler_params=params,
            name=name + ("_later" if backward else "_earlier"),
        )(*args)

    def exchange(whole, axes, peers):
        pieces = whole.reshape(peers, ROWS // peers // 2, 2, LANES)
        return lax.all_to_all(pieces, axes, 0, 0, tiled=True).reshape(ROWS, LANES)

    def scan(whole, backward):
        plane = ("x", "c", "space")
        pieces = exchange(whole, plane, X * CORES * SPACE)
        shapes = (whole_shape, plane_shape, plane_shape)
        lines, edge, both = small(plane_kernel, backward, "plane", shapes, pieces)
        lines = exchange(lines, "z", Z)
        frames = small(frame_kernel, backward, "frame", whole_shape, lines, edge, both)
        return exchange(frames, plane, X * CORES * SPACE)

    blocks = pl.pallas_call(
        block_kernel,
        in_specs=[hbm, hbm],
        out_specs=vmem,
        out_shape=whole_shape,
        scratch_shapes=[rows_scratch, rows_scratch, pltpu.SemaphoreType.DMA((4,))],
        compiler_params=pltpu.CompilerParams(vmem_limit_bytes=60 * BYTES),
        name="blocks",
    )(keys, values)
    state = scan(blocks, False)
    grad_query, adjoint = pl.pallas_call(
        query_kernel,
        in_specs=[vmem] * 3,
        out_specs=(hbm, vmem),
        out_shape=(rows_shape, whole_shape),
        scratch_shapes=[
            rows_scratch,
            pltpu.VMEM((queries.shape[1], 2 * queries.shape[2]), jnp.bfloat16),
            pltpu.SemaphoreType.DMA((len(ENDS),)),
        ],
        compiler_params=params,
        name="queries",
    )(queries, cotangent, state)
    later = scan(adjoint, True)
    grad_key, grad_value = pl.pallas_call(
        key_kernel,
        in_specs=[vmem] * 3,
        out_specs=(hbm, hbm),
        out_shape=(rows_shape, rows_shape),
        scratch_shapes=[rows_scratch, rows_scratch, pltpu.SemaphoreType.DMA((2 * GROUPS,))],
        compiler_params=params,
        name="keys",
    )(keys, values, later)
    return (grad_query, grad_key, grad_value)


def solution(mesh):
    split = Mesh(mesh.devices.reshape(X, Z, CORES, SPACE), ("x", "z", "c", "space"))
    placed = P(("x", "z", "c"), "space", None)
    return jax.shard_map(
        shards,
        mesh=split,
        in_specs=(placed,) * 4,
        out_specs=(placed,) * 3,
        check_vma=False,
    )
```
